32 devices in a mesh: grp: 4 (over z), tile: 8 (over y, x, core).
Axes of the slice: x: 2, y: 2, z: 4, core: 2. Of those that a mesh axis runs over, the one named last changes fastest.
Arguments:
- latent: float32 [512, 128], P(('grp', 'tile')), may hold values from -6 to 6
- momentum: float32 [512, 128], P(('grp', 'tile')), may hold values from -6 to 6
- observed: float32 [512, 128], P(('grp', 'tile')), may hold values from -8 to 8
- nugget: float32 [512, 128], P(('grp', 'tile')), may hold values from 0.25 to 2
- cond_weights: float32 [512, 128, 256], P(('grp', 'tile')), may hold values from -0.375 to 0.375
- whiten: float32 [512, 128, 128], P(('grp', 'tile')), may hold values from -4 to 4
- slot_of_rank: int32 [512], replicated, may hold values from 0 to 511, as said below
- neighbours: int32 [512, 2], P(('grp', 'tile')), may hold values from 0 to 479, as said below
Outputs:
- moved: float32 [512, 128], P(('grp', 'tile'))
- new_momentum: float32 [512, 128], P(('grp', 'tile'))
The draws below stay inside these ranges and needn't reach their ends.
Inputs may be any that keep to these rules, and one draw needn't show every extreme that they name: `slot_of_rank`: A permutation of the 512 slots; slot s is place s % 16 of device s // 16 in the order of grp then tile. Ranks below 64 are coarse blocks: each device holds exactly 2 of them, in its first 2 places. `neighbours`: both entries are distinct ranks lower than the block's own, except that the block of rank 0 lists 0 twice and the block of rank 1 lists 0 and 1; an entry equal to the block's own rank counts as absent. The first entry is always a coarse rank; the second is a coarse rank or the rank of a block held by the same device or by the device one tile index lower or higher in the same group. The block of rank 512 - 1 names rank 512 - 33 as its second entry.
All inputs are finite; a program needn't handle non-finite values.
Results may differ from the reference program's by a relative error of at most 0.00009.
Values sent between devices are 32-bit elements; how exact they have to be, the bound alone decides.
A program may use at most 64 MiB of HBM per device.

```python
import math
import jax
import jax.numpy as jnp
from jax import lax

B = 128
COND = 256
BLK_DEV = 16
COARSE_DEV = 2
DEVS = 32
TILES = 8
NBLK = 512
NCOARSE = 64


def layout_draw(key):
    keys = jax.random.split(jax.random.fold_in(key, 7), 9)
    fine_levels = BLK_DEV - COARSE_DEV
    coarse_order = jax.random.permutation(keys[0], NCOARSE).astype(jnp.int32)
    coarse_slot = coarse_order // COARSE_DEV * BLK_DEV + coarse_order % COARSE_DEV
    places = jax.vmap(lambda one: jax.random.permutation(one, fine_levels))(jax.random.split(keys[1], DEVS))
    fine_ids = jnp.arange(NBLK - NCOARSE, dtype=jnp.int32)
    fine_level = fine_ids // DEVS
    fine_device = fine_ids % DEVS
    fine_slot = fine_device * BLK_DEV + COARSE_DEV + places[fine_device, fine_level].astype(jnp.int32)
    slot_of_rank = jnp.concatenate([coarse_slot, fine_slot]).astype(jnp.int32)
    rank_ids = jnp.arange(NBLK, dtype=jnp.int32)
    upper_rank = jnp.maximum(rank_ids, 2)
    first_coarse = jax.random.randint(keys[2], (NBLK,), 0, upper_rank)
    second_coarse = (first_coarse + 1 + jax.random.randint(keys[3], (NBLK,), 0, upper_rank - 1)) % upper_rank
    hot_pick = jax.random.randint(keys[4], (NBLK,), 0, NCOARSE) * jax.random.randint(keys[5], (NBLK,), 0, NCOARSE) // NCOARSE
    other_pick = (hot_pick + 1 + jax.random.randint(keys[6], (NBLK,), 0, NCOARSE - 1)) % NCOARSE
    level = jnp.maximum(rank_ids - NCOARSE, 0) // DEVS
    device = jnp.maximum(rank_ids - NCOARSE, 0) % DEVS
    early_level = jax.random.randint(keys[7], (NBLK,), 0, jnp.maximum(level, 1))
    offset_tile = jax.random.randint(keys[8], (NBLK,), 0, 3) - 1
    tile_now = device % TILES
    inside = (tile_now + offset_tile >= 0) & (tile_now + offset_tile < TILES)
    offset_tile = jnp.where(inside, offset_tile, 0)
    fine_second = NCOARSE + early_level * DEVS + device + offset_tile
    fine_second = jnp.where(level == 0, other_pick, fine_second)
    fine_second = jnp.where(rank_ids == NBLK - 1, NBLK - DEVS - 1, fine_second)
    first_entry = jnp.where(rank_ids < NCOARSE, first_coarse, hot_pick)
    second_entry = jnp.where(rank_ids < NCOARSE, second_coarse, fine_second)
    first_entry = jnp.where(rank_ids < 2, 0, first_entry)
    second_entry = jnp.where(rank_ids < 2, rank_ids, second_entry)
    by_rank = jnp.stack([first_entry, second_entry], axis=1).astype(jnp.int32)
    by_slot = jnp.zeros((NBLK, 2), jnp.int32).at[slot_of_rank].set(by_rank)
    return (slot_of_rank, by_slot)


def draw_slot_of_rank(key, part):
    return layout_draw(key)[0]


def draw_neighbours(key, part):
    return layout_draw(key)[1]


def draw_whiten(key, part):
    keys = jax.random.split(jax.random.fold_in(key, 11), 2)
    diagonal = jnp.exp(jax.random.uniform(keys[0], (NBLK, B), jnp.float32, math.log(0.5), math.log(2.0)))
    lower_part = jnp.clip(jax.random.normal(keys[1], (NBLK, B, B), jnp.float32), -4.0, 4.0) * (0.6 / math.sqrt(B))
    strict = jnp.tril(jnp.ones((B, B), jnp.float32), -1)
    result = lower_part * strict[None] + diagonal[:, :, None] * jnp.eye(B, dtype=jnp.float32)[None]
    return result


def levels(key, extent, pieces, least, largest):
    def one(axis_at, shards_of):
        steps = jax.random.uniform(jax.random.fold_in(jax.random.fold_in(key, 6), axis_at), (shards_of,), jnp.float32, least / len(pieces), largest / len(pieces))
        return jnp.repeat(jnp.exp(steps), extent[axis_at] // shards_of).reshape((-1,) + (1,) * (len(extent) - axis_at - 1))

    factor_of = one(*pieces[0])
    for cut in pieces[1:]:
        factor_of = factor_of * one(*cut)
    return factor_of


def centred(rng, dims, spread, most, cuts=(), held_as=jnp.bfloat16):
    loudness = levels(rng, dims, cuts, -0.22, 0.18) if cuts else 1.0
    entries = jax.random.normal(rng, dims, jnp.float32) * spread * loudness
    return jnp.minimum(jnp.maximum(entries, -most), most).astype(held_as)


def setup_inputs(seed: int = 0) -> dict:
    seeds = jax.random.split(jax.random.key(seed), 9)
    return {
        "latent": centred(seeds[0], (NBLK, B), 1.0, 6.0, ((0, 32),), jnp.float32),
        "momentum": centred(seeds[1], (NBLK, B), 1.0, 6.0, ((0, 32),), jnp.float32),
        "observed": centred(seeds[2], (NBLK, B), 1.5, 8.0, ((0, 32),), jnp.float32),
        "nugget": jnp.clip(jnp.exp(math.log(2.0) - 2.0794415 * jax.random.uniform(seeds[3], (NBLK, B), jnp.float32) ** levels(seeds[3], (NBLK, B), ((0, 32),), -0.2, 0.2)), 0.25, 2.0),
        "cond_weights": centred(seeds[4], (NBLK, B, COND), COND ** -0.5, 0.375, ((0, 32),), jnp.float32),
        "whiten": draw_whiten(jax.random.fold_in(seeds[8], 71), 0),
        "slot_of_rank": draw_slot_of_rank(jax.random.fold_in(seeds[8], 71), 0),
        "neighbours": draw_neighbours(jax.random.fold_in(seeds[8], 71), 0),
    }


leap_step = 0.25


def gradient(latent_now, observed, nugget, cond_weights, whiten, slot_of_rank, neighbours):
    total = latent_now.shape[0]
    own_rank = jnp.zeros((total,), jnp.int32).at[slot_of_rank].set(jnp.arange(total, dtype=jnp.int32))
    present = (neighbours != own_rank[:, None]).astype(latent_now.dtype)
    cond_slots = slot_of_rank[neighbours]
    cond_values = (latent_now[cond_slots] * present[:, :, None]).reshape(total, -1)
    cond_mean = jnp.einsum("bij,bj->bi", cond_weights, cond_values, precision=lax.Precision.HIGHEST)
    whitened = jnp.einsum("bij,bj->bi", whiten, latent_now - cond_mean, precision=lax.Precision.HIGHEST)
    own_term = jnp.einsum("bji,bj->bi", whiten, whitened, precision=lax.Precision.HIGHEST)
    push_back = jnp.einsum("bji,bj->bi", cond_weights, own_term, precision=lax.Precision.HIGHEST)
    push_back = push_back.reshape(total, 2, -1) * present[:, :, None]
    pulled = jnp.zeros_like(latent_now).at[cond_slots.reshape(-1)].add(push_back.reshape(total * 2, -1))
    return own_term + (latent_now - observed) / nugget - pulled


def reference(latent, momentum, observed, nugget, cond_weights, whiten, slot_of_rank, neighbours):
    start_grad = gradient(latent, observed, nugget, cond_weights, whiten, slot_of_rank, neighbours)
    half_momentum = momentum - 0.5 * leap_step * start_grad
    moved = latent + leap_step * half_momentum
    end_grad = gradient(moved, observed, nugget, cond_weights, whiten, slot_of_rank, neighbours)
    new_momentum = half_momentum - 0.5 * leap_step * end_grad
    return moved, new_momentum
```

```python
import functools

import jax
import jax.numpy as jnp
from jax import lax
from jax.experimental import pallas as pl
from jax.experimental.pallas import tpu as pltpu
from jax.sharding import PartitionSpec as P

COARSE_DEV = 2
ROWS = 8

leap_step = 0.25

MESH = pl.DeviceIdType.MESH
HIGHEST = lax.Precision.HIGHEST


def kernel(
    ngrp,
    ntile,
    latent_ref,
    momentum_ref,
    observed_ref,
    nugget_ref,
    cond_hbm,
    whiten_hbm,
    slot_ref,
    neigh_ref,
    moved_ref,
    newmom_ref,
    cond,
    whit,
    both,
    table,
    sent,
    landed,
    near,
    push,
    own,
    index,
    load_sem,
    send_sem,
    recv_sem,
    near_sem,
):
    blocks, width = latent_ref.shape
    devices = ngrp * ntile
    grp = lax.axis_index("grp")
    tile = lax.axis_index("tile")
    me = grp * ntile + tile
    halo = devices * ROWS
    absent = halo + 3 * blocks
    above = (grp, lax.rem(tile + 1, ntile))
    below = (grp, lax.rem(tile + ntile - 1, ntile))

    def peer(step):
        flat = lax.rem(me + step, devices)
        return flat, (flat // ntile, lax.rem(flat, ntile))

    loads = []
    pieces = load_sem.shape[1]
    part = blocks // pieces
    for i in range(pieces):
        rows = pl.ds(i * part, part)
        loads.append(
            (
                pltpu.make_async_copy(whiten_hbm.at[rows], whit.at[rows], load_sem.at[0, i]),
                pltpu.make_async_copy(cond_hbm.at[rows], cond.at[rows], load_sem.at[1, i]),
            )
        )
    for pair in loads:
        for copy in pair:
            copy.start()

    barrier = pltpu.get_barrier_semaphore()

    def greet(step, carry):
        pl.semaphore_signal(barrier, inc=1, device_id=peer(step)[1], device_id_type=MESH)
        return carry

    lax.fori_loop(1, devices, greet, 0)

    lanes = lax.broadcasted_iota(jnp.int32, (1, 6 * blocks), 1) % (2 * blocks)
    places = jnp.full((1, 6 * blocks), -1, jnp.int32)
    for s in range(blocks):
        for k in range(2):
            rank = neigh_ref[s, k]
            slot = slot_ref[rank]
            owner = slot // blocks
            place = lax.rem(slot, blocks)
            row = jnp.where(
                rank < COARSE_DEV * devices,
                owner * ROWS + place,
                halo + (owner - me + 1) * blocks + place,
            )
            row = jnp.where(slot == me * blocks + s, absent, row)
            index[k * blocks + s] = row
            places = jnp.where(lanes == k * blocks + s, row, places)
    hot = (lax.broadcasted_iota(jnp.int32, (absent, 6 * blocks), 0) == places)
    hot = hot.astype(jnp.float32).astype(jnp.bfloat16)
    for turn in range(2):
        table[turn, absent : absent + ROWS] = jnp.zeros((ROWS, width), jnp.float32)

    pl.semaphore_wait(barrier, devices - 1)

    def spread(turn, values):
        sends = []
        for side, (to, row) in enumerate(((above, halo), (below, halo + 2 * blocks))):
            copy = pltpu.make_async_remote_copy(
                src_ref=values,
                dst_ref=table.at[turn, pl.ds(row, blocks)],
                send_sem=near_sem.at[turn, 0, side],
                recv_sem=near_sem.at[turn, 1, side],
                device_id=to,
                device_id_type=MESH,
            )
            copy.start()
            sends.append(copy)

        def send(step, carry):
            pltpu.make_async_remote_copy(
                src_ref=values.at[pl.ds(0, COARSE_DEV)],
                dst_ref=table.at[turn, pl.ds(pl.multiple_of(me * ROWS, ROWS), COARSE_DEV)],
                send_sem=send_sem.at[turn],
                recv_sem=recv_sem.at[turn],
                device_id=peer(step)[1],
                device_id_type=MESH,
            ).start()
            return carry

        lax.fori_loop(1, devices, send, 0)
        table[turn, pl.ds(pl.multiple_of(me * ROWS, ROWS), COARSE_DEV)] = values[:COARSE_DEV]
        table[turn, halo + blocks : halo + 2 * blocks] = values[...]
        return sends

    def give(turn):
        sends = []
        for side, (to, row) in enumerate(((above, halo + 2 * blocks), (below, halo))):
            copy = pltpu.make_async_remote_copy(
                src_ref=sent.at[turn - 2, pl.ds(row, blocks)],
                dst_ref=near.at[turn - 2, side],
                send_sem=near_sem.at[turn, 0, side],
                recv_sem=near_sem.at[turn, 1, side],
                device_id=to,
                device_id_type=MESH,
            )
            copy.start()
            sends.append(copy)

        def send(step, carry):
            flat, to = peer(step)
            pltpu.make_async_remote_copy(
                src_ref=sent.at[turn - 2, pl.ds(pl.multiple_of(flat * ROWS, ROWS), COARSE_DEV)],
                dst_ref=landed.at[turn - 2, pl.ds(pl.multiple_of(me * ROWS, ROWS), COARSE_DEV)],
                send_sem=send_sem.at[turn],
                recv_sem=recv_sem.at[turn],
                device_id=to,
                device_id_type=MESH,
            ).start()
            return carry

        lax.fori_loop(1, devices, send, 0)
        mine = pl.ds(pl.multiple_of(me * ROWS, ROWS), ROWS)
        landed[turn - 2, mine] = sent[turn - 2, mine]
        return sends

    def arrive(turn, buffer, sends):
        for copy in sends:
            copy.wait_recv()
        amount = buffer.at[pl.ds(0, (devices - 1) * COARSE_DEV)]
        pltpu.make_async_copy(amount, amount, recv_sem.at[turn]).wait()

    def drain(turn, buffer, sends):
        for copy in sends:
            copy.wait_send()
        amount = buffer.at[pl.ds(0, (devices - 1) * COARSE_DEV)]
        pltpu.make_async_copy(amount, amount, send_sem.at[turn]).wait()

    first = spread(0, latent_ref)

    for i, pair in enumerate(loads):
        for copy in pair:
            copy.wait()
        for b in range(i * part, (i + 1) * part):
            square = lax.dot_general(
                whit[b], whit[b], (((0,), (0,)), ((), ())),
                precision=HIGHEST, preferred_element_type=jnp.float32,
            )
            both[b, :, :width] = square
            both[b, :, width:] = jnp.dot(
                square, cond[b], precision=HIGHEST, preferred_element_type=jnp.float32
            )

    diagonal = lax.broadcasted_iota(jnp.int32, (width, width), 0) == lax.broadcasted_iota(
        jnp.int32, (width, width), 1
    )

    def pushes(turn, values):
        for b in range(blocks):
            c0 = table[turn, pl.ds(index[b], 1), :]
            c1 = table[turn, pl.ds(index[blocks + b], 1), :]
            spreadout = jnp.where(diagonal, values[b : b + 1, :], 0.0)
            spreadout -= cond[b, :, :width] * c0 + cond[b, :, width:] * c1
            rest = jnp.sum(spreadout, axis=1, keepdims=True)
            out = jnp.sum(both[b] * rest, axis=0, keepdims=True)
            own[b : b + 1, :] = out[:, :width]
            push[b : b + 1, :] = out[:, width : 2 * width]
            push[blocks + b : blocks + b + 1, :] = out[:, 2 * width :]
        rest = push[...]
        split = []
        for _ in range(3):
            piece = rest.astype(jnp.bfloat16)
            split.append(piece)
            rest = rest - piece.astype(jnp.float32)
        sent[turn] = jnp.dot(
            hot, jnp.concatenate(split, axis=0), preferred_element_type=jnp.float32
        )

    def pulled(turn):
        total = landed[turn].reshape(devices, ROWS, width).sum(axis=0)
        row = lax.broadcasted_iota(jnp.int32, (ROWS, width), 0)
        total = jnp.where(row < COARSE_DEV, total, 0.0)
        total = jnp.concatenate(
            [total, jnp.zeros((blocks - ROWS, width), jnp.float32)], axis=0
        )
        return total + sent[turn, halo + blocks : halo + 2 * blocks] + near[turn, 0] + near[turn, 1]

    latent = latent_ref[...]
    arrive(0, table.at[0], first)
    pushes(0, latent_ref)
    second = give(2)
    known = own[...] + (latent - observed_ref[...]) / nugget_ref[...]
    arrive(2, landed.at[0], second)
    half = momentum_ref[...] - 0.5 * leap_step * (known - pulled(0))
    moved = latent + leap_step * half
    moved_ref[...] = moved
    third = spread(1, moved_ref)
    arrive(1, table.at[1], third)
    pushes(1, moved_ref)
    fourth = give(3)
    known = own[...] + (moved - observed_ref[...]) / nugget_ref[...]
    arrive(3, landed.at[1], fourth)
    newmom_ref[...] = half - 0.5 * leap_step * (known - pulled(1))
    drain(0, table.at[0], first)
    drain(2, landed.at[0], second)
    drain(1, table.at[1], third)
    drain(3, landed.at[1], fourth)


def on_device(latent, momentum, observed, nugget, cond_weights, whiten, slot_of_rank, neighbours):
    ngrp, ntile = lax.axis_size("grp"), lax.axis_size("tile")
    blocks, width = latent.shape
    devices = ngrp * ntile
    rows = devices * ROWS + 3 * blocks
    f32 = jnp.float32
    vmem = pl.BlockSpec(memory_space=pltpu.VMEM)
    smem = pl.BlockSpec(memory_space=pltpu.SMEM)
    anywhere = pl.BlockSpec(memory_space=pl.ANY)
    return pl.pallas_call(
        functools.partial(kernel, ngrp, ntile),
        out_shape=[jax.ShapeDtypeStruct((blocks, width), f32)] * 2,
        in_specs=[vmem] * 4 + [anywhere] * 2 + [smem] * 2,
        out_specs=[vmem] * 2,
        scratch_shapes=[
            pltpu.VMEM(cond_weights.shape, f32),
            pltpu.VMEM(whiten.shape, f32),
            pltpu.VMEM((blocks, width, 3 * width), f32),
            pltpu.VMEM((2, rows + ROWS, width), f32),
            pltpu.VMEM((2, rows, width), f32),
            pltpu.VMEM((2, devices * ROWS, width), f32),
            pltpu.VMEM((2, 2, blocks, width), f32),
            pltpu.VMEM((2 * blocks, width), f32),
            pltpu.VMEM((blocks, width), f32),
            pltpu.SMEM((2 * blocks,), jnp.int32),
            pltpu.SemaphoreType.DMA((2, 4)),
            pltpu.SemaphoreType.DMA((4,)),
            pltpu.SemaphoreType.DMA((4,)),
            pltpu.SemaphoreType.DMA((4, 2, 2)),
        ],
        compiler_params=pltpu.CompilerParams(
            collective_id=0, has_side_effects=True, vmem_limit_bytes=40 * 1024 * 1024
        ),
    )(latent, momentum, observed, nugget, cond_weights, whiten, slot_of_rank, neighbours)


def solution(mesh):
    split = P(("grp", "tile"), None)
    cube = P(("grp", "tile"), None, None)
    return jax.shard_map(
        on_device,
        mesh=mesh,
        in_specs=(split, split, split, split, cube, cube, P(), split),
        out_specs=(split, split),
        check_vma=False,
    )
```

```python
import functools

import jax
import jax.numpy as jnp
from jax import lax
from jax.experimental import pallas as pl
from jax.experimental.pallas import tpu as pltpu
from jax.sharding import PartitionSpec as P

COARSE_DEV = 2
ROWS = 8

leap_step = 0.25

MESH = pl.DeviceIdType.MESH


def halves(x):
    high = x.astype(jnp.bfloat16)
    return high, (x - high.astype(jnp.float32)).astype(jnp.bfloat16)


def kernel(
    ngrp,
    ntile,
    latent_hbm,
    momentum_hbm,
    observed_hbm,
    nugget_hbm,
    cond_hbm,
    whiten_hbm,
    slot_hbm,
    neigh_hbm,
    moved_ref,
    newmom_ref,
    latent_ref,
    momentum_ref,
    observed_ref,
    nugget_ref,
    slot_ref,
    neigh_ref,
    cond,
    whit,
    both,
    table,
    sent,
    landed,
    near,
    push,
    own,
    index,
    small_sem,
    load_sem,
    send_sem,
    recv_sem,
    near_sem,
):
    blocks, width = latent_ref.shape
    devices = ngrp * ntile
    grp = lax.axis_index("grp")
    tile = lax.axis_index("tile")
    me = grp * ntile + tile
    halo = devices * ROWS
    absent = halo + 3 * blocks
    above = (grp, lax.rem(tile + 1, ntile))
    below = (grp, lax.rem(tile + ntile - 1, ntile))

    def peer(step):
        flat = lax.rem(me + step, devices)
        return flat, (flat // ntile, lax.rem(flat, ntile))

    small = [
        pltpu.make_async_copy(source, target, small_sem.at[i])
        for i, (source, target) in enumerate(
            (
                (neigh_hbm, neigh_ref),
                (slot_hbm, slot_ref),
                (latent_hbm, latent_ref),
                (momentum_hbm, momentum_ref),
                (observed_hbm, observed_ref),
                (nugget_hbm, nugget_ref),
            )
        )
    ]
    for copy in small:
        copy.start()
    loads = []
    pieces = load_sem.shape[1]
    part = blocks // pieces
    for i in range(pieces):
        rows = pl.ds(i * part, part)
        loads.append(
            (
                pltpu.make_async_copy(whiten_hbm.at[rows], whit.at[rows], load_sem.at[0, i]),
                pltpu.make_async_copy(cond_hbm.at[rows], cond.at[rows], load_sem.at[1, i]),
            )
        )
    for pair in loads:
        for copy in pair:
            copy.start()

    barrier = pltpu.get_barrier_semaphore()

    def greet(step, carry):
        pl.semaphore_signal(barrier, inc=1, device_id=peer(step)[1], device_id_type=MESH)
        return carry

    lax.fori_loop(1, devices, greet, 0)

    small[0].wait()
    small[1].wait()

    lanes = lax.broadcasted_iota(jnp.int32, (1, 6 * blocks), 1) % (2 * blocks)
    places = jnp.full((1, 6 * blocks), -1, jnp.int32)
    for s in range(blocks):
        for k in range(2):
            rank = neigh_ref[k, s]
            slot = slot_ref[rank]
            owner = slot // blocks
            place = lax.rem(slot, blocks)
            row = jnp.where(
                rank < COARSE_DEV * devices,
                owner * ROWS + place,
                halo + (owner - me + 1) * blocks + place,
            )
            row = jnp.where(slot == me * blocks + s, absent, row)
            index[k * blocks + s] = row
            places = jnp.where(lanes == k * blocks + s, row, places)
    hot = (lax.broadcasted_iota(jnp.int32, (absent, 6 * blocks), 0) == places)
    hot = hot.astype(jnp.float32).astype(jnp.bfloat16)
    for turn in range(2):
        table[turn, absent : absent + ROWS] = jnp.zeros((ROWS, width), jnp.float32)

    for copy in small[2:]:
        copy.wait()
    pl.semaphore_wait(barrier, devices - 1)

    def spread(turn, values):
        sends = []
        for side, (to, row) in enumerate(((above, halo), (below, halo + 2 * blocks))):
            copy = pltpu.make_async_remote_copy(
                src_ref=values,
                dst_ref=table.at[turn, pl.ds(row, blocks)],
                send_sem=near_sem.at[turn, 0, side],
                recv_sem=near_sem.at[turn, 1, side],
                device_id=to,
                device_id_type=MESH,
            )
            copy.start()
            sends.append(copy)

        def send(step, carry):
            pltpu.make_async_remote_copy(
                src_ref=values.at[pl.ds(0, COARSE_DEV)],
                dst_ref=table.at[turn, pl.ds(pl.multiple_of(me * ROWS, ROWS), COARSE_DEV)],
                send_sem=send_sem.at[turn],
                recv_sem=recv_sem.at[turn],
                device_id=peer(step)[1],
                device_id_type=MESH,
            ).start()
            return carry

        lax.fori_loop(1, devices, send, 0)
        table[turn, pl.ds(pl.multiple_of(me * ROWS, ROWS), COARSE_DEV)] = values[:COARSE_DEV]
        table[turn, halo + blocks : halo + 2 * blocks] = values[...]
        return sends

    def give(turn):
        sends = []
        for side, (to, row) in enumerate(((above, halo + 2 * blocks), (below, halo))):
            copy = pltpu.make_async_remote_copy(
                src_ref=sent.at[turn - 2, pl.ds(row, blocks)],
                dst_ref=near.at[turn - 2, side],
                send_sem=near_sem.at[turn, 0, side],
                recv_sem=near_sem.at[turn, 1, side],
                device_id=to,
                device_id_type=MESH,
            )
            copy.start()
            sends.append(copy)

        def send(step, carry):
            flat, to = peer(step)
            pltpu.make_async_remote_copy(
                src_ref=sent.at[turn - 2, pl.ds(pl.multiple_of(flat * ROWS, ROWS), COARSE_DEV)],
                dst_ref=landed.at[turn - 2, pl.ds(pl.multiple_of(me * ROWS, ROWS), COARSE_DEV)],
                send_sem=send_sem.at[turn],
                recv_sem=recv_sem.at[turn],
                device_id=to,
                device_id_type=MESH,
            ).start()
            return carry

        lax.fori_loop(1, devices, send, 0)
        mine = pl.ds(pl.multiple_of(me * ROWS, ROWS), ROWS)
        landed[turn - 2, mine] = sent[turn - 2, mine]
        return sends

    def arrive(turn, buffer, sends):
        for copy in sends:
            copy.wait_recv()
        amount = buffer.at[pl.ds(0, (devices - 1) * COARSE_DEV)]
        pltpu.make_async_copy(amount, amount, recv_sem.at[turn]).wait()

    def drain(turn, buffer, sends):
        for copy in sends:
            copy.wait_send()
        amount = buffer.at[pl.ds(0, (devices - 1) * COARSE_DEV)]
        pltpu.make_async_copy(amount, amount, send_sem.at[turn]).wait()

    first = spread(0, latent_ref)

    for i, pair in enumerate(loads):
        for copy in pair:
            copy.wait()
        for b in range(i * part, (i + 1) * part):
            high, low = halves(whit[b])
            square = lax.dot_general(
                jnp.concatenate([high, high, low], axis=0),
                jnp.concatenate([high, low, high], axis=0),
                (((0,), (0,)), ((), ())),
                preferred_element_type=jnp.float32,
            )
            both[b, :, :width] = square
            left_high, left_low = halves(square)
            high, low = halves(cond[b])
            both[b, :, width:] = jnp.dot(
                jnp.concatenate([left_high, left_high, left_low], axis=1),
                jnp.concatenate([high, low, high], axis=0),
                preferred_element_type=jnp.float32,
            )

    diagonal = lax.broadcasted_iota(jnp.int32, (width, width), 0) == lax.broadcasted_iota(
        jnp.int32, (width, width), 1
    )

    def pushes(turn, values):
        for b in range(blocks):
            c0 = table[turn, pl.ds(index[b], 1), :]
            c1 = table[turn, pl.ds(index[blocks + b], 1), :]
            spreadout = jnp.where(diagonal, values[b : b + 1, :], 0.0)
            spreadout -= cond[b, :, :width] * c0 + cond[b, :, width:] * c1
            rest = jnp.sum(spreadout, axis=1, keepdims=True)
            out = jnp.sum(both[b] * rest, axis=0, keepdims=True)
            own[b : b + 1, :] = out[:, :width]
            push[b : b + 1, :] = out[:, width : 2 * width]
            push[blocks + b : blocks + b + 1, :] = out[:, 2 * width :]
        rest = push[...]
        split = []
        for _ in range(3):
            piece = rest.astype(jnp.bfloat16)
            split.append(piece)
            rest = rest - piece.astype(jnp.float32)
        sent[turn] = jnp.dot(
            hot, jnp.concatenate(split, axis=0), preferred_element_type=jnp.float32
        )

    def pulled(turn):
        total = landed[turn].reshape(devices, ROWS, width).sum(axis=0)
        row = lax.broadcasted_iota(jnp.int32, (ROWS, width), 0)
        total = jnp.where(row < COARSE_DEV, total, 0.0)
        total = jnp.concatenate(
            [total, jnp.zeros((blocks - ROWS, width), jnp.float32)], axis=0
        )
        return total + sent[turn, halo + blocks : halo + 2 * blocks] + near[turn, 0] + near[turn, 1]

    latent = latent_ref[...]
    arrive(0, table.at[0], first)
    pushes(0, latent_ref)
    second = give(2)
    known = own[...] + (latent - observed_ref[...]) / nugget_ref[...]
    arrive(2, landed.at[0], second)
    half = momentum_ref[...] - 0.5 * leap_step * (known - pulled(0))
    moved = latent + leap_step * half
    moved_ref[...] = moved
    third = spread(1, moved_ref)
    arrive(1, table.at[1], third)
    pushes(1, moved_ref)
    fourth = give(3)
    known = own[...] + (moved - observed_ref[...]) / nugget_ref[...]
    arrive(3, landed.at[1], fourth)
    newmom_ref[...] = half - 0.5 * leap_step * (known - pulled(1))
    drain(0, table.at[0], first)
    drain(2, landed.at[0], second)
    drain(1, table.at[1], third)
    drain(3, landed.at[1], fourth)


def on_device(latent, momentum, observed, nugget, cond_weights, whiten, slot_of_rank, neighbours):
    ngrp, ntile = lax.axis_size("grp"), lax.axis_size("tile")
    blocks, width = latent.shape
    devices = ngrp * ntile
    rows = devices * ROWS + 3 * blocks
    f32 = jnp.float32
    vmem = pl.BlockSpec(memory_space=pltpu.VMEM)
    anywhere = pl.BlockSpec(memory_space=pltpu.HBM)
    return pl.pallas_call(
        functools.partial(kernel, ngrp, ntile),
        out_shape=[jax.ShapeDtypeStruct((blocks, width), f32)] * 2,
        in_specs=[anywhere] * 8,
        out_specs=[vmem] * 2,
        scratch_shapes=[
            *[pltpu.VMEM((blocks, width), f32)] * 4,
            pltpu.SMEM(slot_of_rank.shape, jnp.int32),
            pltpu.SMEM((2, blocks), jnp.int32),
            pltpu.VMEM(cond_weights.shape, f32),
            pltpu.VMEM(whiten.shape, f32),
            pltpu.VMEM((blocks, width, 3 * width), f32),
            pltpu.VMEM((2, rows + ROWS, width), f32),
            pltpu.VMEM((2, rows, width), f32),
            pltpu.VMEM((2, devices * ROWS, width), f32),
            pltpu.VMEM((2, 2, blocks, width), f32),
            pltpu.VMEM((2 * blocks, width), f32),
            pltpu.VMEM((blocks, width), f32),
            pltpu.SMEM((2 * blocks,), jnp.int32),
            pltpu.SemaphoreType.DMA((6,)),
            pltpu.SemaphoreType.DMA((2, 4)),
            pltpu.SemaphoreType.DMA((4,)),
            pltpu.SemaphoreType.DMA((4,)),
            pltpu.SemaphoreType.DMA((4, 2, 2)),
        ],
        compiler_params=pltpu.CompilerParams(
            collective_id=0, has_side_effects=True, vmem_limit_bytes=60 * 1024 * 1024
        ),
    )(latent, momentum, observed, nugget, cond_weights, whiten, slot_of_rank, neighbours.T)


def solution(mesh):
    split = P(("grp", "tile"), None)
    cube = P(("grp", "tile"), None, None)
    return jax.shard_map(
        on_device,
        mesh=mesh,
        in_specs=(split, split, split, split, cube, cube, P(), split),
        out_specs=(split, split),
        check_vma=False,
    )
```

```python
import functools

import jax
import jax.numpy as jnp
from jax import lax
from jax.experimental import pallas as pl
from jax.experimental.pallas import tpu as pltpu
from jax.sharding import PartitionSpec as P

COARSE_DEV = 2
ROWS = 8

leap_step = 0.25

MESH = pl.DeviceIdType.MESH


def halves(x):
    high = x.astype(jnp.bfloat16)
    return high, (x - high.astype(jnp.float32)).astype(jnp.bfloat16)


def kernel(
    ngrp,
    ntile,
    latent_hbm,
    momentum_hbm,
    observed_hbm,
    nugget_hbm,
    cond_hbm,
    whiten_hbm,
    slot_hbm,
    neigh_hbm,
    half_ref,
    grad_ref,
    latent_ref,
    momentum_ref,
    observed_ref,
    nugget_ref,
    slot_ref,
    neigh_ref,
    cond,
    whit,
    both,
    table,
    sent,
    landed,
    near,
    push,
    own,
    fine,
    coarse,
    index,
    small_sem,
    load_sem,
    send_sem,
    recv_sem,
    near_sem,
):
    blocks, width = latent_ref.shape
    devices = ngrp * ntile
    grp = lax.axis_index("grp")
    tile = lax.axis_index("tile")
    me = grp * ntile + tile
    halo = devices * ROWS
    absent = halo + 3 * blocks
    above = (grp, lax.rem(tile + 1, ntile))
    below = (grp, lax.rem(tile + ntile - 1, ntile))

    def everyone(act):
        if devices <= 64:
            groups = [lax.rem(grp + a, ngrp) for a in range(ngrp)]
            tiles = [lax.rem(tile + b, ntile) for b in range(ntile)]
            for a in [*range(1, ngrp), 0]:
                for b in reversed(range(ntile)):
                    if a or b:
                        act(groups[a] * ntile + tiles[b], (groups[a], tiles[b]))
        else:

            def body(step, carry):
                flat = lax.rem(me + step, devices)
                act(flat, (flat // ntile, lax.rem(flat, ntile)))
                return carry

            lax.fori_loop(1, devices, body, 0)

    small = [
        pltpu.make_async_copy(source, target, small_sem.at[i])
        for i, (source, target) in enumerate(
            (
                (neigh_hbm, neigh_ref),
                (slot_hbm, slot_ref),
                (latent_hbm, latent_ref),
                (momentum_hbm, momentum_ref),
                (observed_hbm, observed_ref),
                (nugget_hbm, nugget_ref),
            )
        )
    ]
    for copy in small:
        copy.start()
    loads = []
    pieces = load_sem.shape[1]
    part = blocks // pieces
    for i in range(pieces):
        rows = pl.ds(i * part, part)
        loads.append(
            (
                pltpu.make_async_copy(whiten_hbm.at[rows], whit.at[rows], load_sem.at[0, i]),
                pltpu.make_async_copy(cond_hbm.at[rows], cond.at[rows], load_sem.at[1, i]),
            )
        )
    for pair in loads:
        for copy in pair:
            copy.start()

    barrier = pltpu.get_barrier_semaphore()

    def greet(flat, to):
        pl.semaphore_signal(barrier, inc=1, device_id=to, device_id_type=MESH)

    everyone(greet)
    pl.semaphore_wait(barrier, devices - 1)

    my_rows = pl.ds(pl.multiple_of(me * ROWS, ROWS), COARSE_DEV)

    def spread_coarse(turn, values):
        def send(flat, to):
            pltpu.make_async_remote_copy(
                src_ref=values,
                dst_ref=table.at[turn, my_rows],
                send_sem=send_sem.at[turn],
                recv_sem=recv_sem.at[turn],
                device_id=to,
                device_id_type=MESH,
            ).start()

        everyone(send)

    def spread_near(turn, values):
        sends = []
        for side, (to, row) in enumerate(((above, halo), (below, halo + 2 * blocks))):
            copy = pltpu.make_async_remote_copy(
                src_ref=values,
                dst_ref=table.at[turn, pl.ds(row, blocks)],
                send_sem=near_sem.at[turn, 0, side],
                recv_sem=near_sem.at[turn, 1, side],
                device_id=to,
                device_id_type=MESH,
            )
            copy.start()
            sends.append(copy)
        return sends

    def give(turn):
        def send(flat, to):
            pltpu.make_async_remote_copy(
                src_ref=sent.at[turn - 2, pl.ds(pl.multiple_of(flat * ROWS, ROWS), COARSE_DEV)],
                dst_ref=landed.at[turn - 2, my_rows],
                send_sem=send_sem.at[turn],
                recv_sem=recv_sem.at[turn],
                device_id=to,
                device_id_type=MESH,
            ).start()

        everyone(send)
        sends = []
        for side, (to, row) in enumerate(((above, halo + 2 * blocks), (below, halo))):
            copy = pltpu.make_async_remote_copy(
                src_ref=sent.at[turn - 2, pl.ds(row, blocks)],
                dst_ref=near.at[turn - 2, side],
                send_sem=near_sem.at[turn, 0, side],
                recv_sem=near_sem.at[turn, 1, side],
                device_id=to,
                device_id_type=MESH,
            )
            copy.start()
            sends.append(copy)
        mine = pl.ds(pl.multiple_of(me * ROWS, ROWS), ROWS)
        landed[turn - 2, mine] = sent[turn - 2, mine]
        return sends

    def arrive_near(sends):
        for copy in sends:
            copy.wait_recv()

    def arrive_coarse(turn, buffer):
        amount = buffer.at[pl.ds(0, (devices - 1) * COARSE_DEV)]
        pltpu.make_async_copy(amount, amount, recv_sem.at[turn]).wait()

    def drain(turn, buffer, sends):
        for copy in sends:
            copy.wait_send()
        amount = buffer.at[pl.ds(0, (devices - 1) * COARSE_DEV)]
        pltpu.make_async_copy(amount, amount, send_sem.at[turn]).wait()

    def keep(turn, values):
        table[turn, my_rows] = values[:COARSE_DEV]
        table[turn, halo + blocks : halo + 2 * blocks] = values

    spread_coarse(0, latent_hbm.at[pl.ds(0, COARSE_DEV)])
    first = spread_near(0, latent_hbm)
    small[0].wait()
    small[1].wait()
    lanes = lax.broadcasted_iota(jnp.int32, (1, 6 * blocks), 1) % (2 * blocks)
    places = jnp.full((1, 6 * blocks), -1, jnp.int32)
    for s in range(blocks):
        for k in range(2):
            rank = neigh_ref[k, s]
            slot = slot_ref[rank]
            owner = slot // blocks
            place = lax.rem(slot, blocks)
            row = jnp.where(
                rank < COARSE_DEV * devices,
                owner * ROWS + place,
                halo + (owner - me + 1) * blocks + place,
            )
            row = jnp.where(slot == me * blocks + s, absent, row)
            index[k * blocks + s] = row
            places = jnp.where(lanes == k * blocks + s, row, places)
    hot = (lax.broadcasted_iota(jnp.int32, (absent, 6 * blocks), 0) == places)
    hot = hot.astype(jnp.float32).astype(jnp.bfloat16)
    for turn in range(2):
        table[turn, absent : absent + ROWS] = jnp.zeros((ROWS, width), jnp.float32)

    for copy in small[2:]:
        copy.wait()
    latent = latent_ref[...]
    keep(0, latent)

    for i, pair in enumerate(loads):
        for copy in pair:
            copy.wait()
        for b in range(i * part, (i + 1) * part):
            high, low = halves(whit[b])
            square = lax.dot_general(
                jnp.concatenate([high, high, low], axis=0),
                jnp.concatenate([high, low, high], axis=0),
                (((0,), (0,)), ((), ())),
                preferred_element_type=jnp.float32,
            )
            both[b, :, :width] = square
            left_high, left_low = halves(square)
            high, low = halves(cond[b])
            both[b, :, width:] = jnp.dot(
                jnp.concatenate([left_high, left_high, left_low], axis=1),
                jnp.concatenate([high, low, high], axis=0),
                preferred_element_type=jnp.float32,
            )

    diagonal = lax.broadcasted_iota(jnp.int32, (width, width), 0) == lax.broadcasted_iota(
        jnp.int32, (width, width), 1
    )

    def pushes(turn, values):
        for b in range(blocks):
            c0 = table[turn, pl.ds(index[b], 1), :]
            c1 = table[turn, pl.ds(index[blocks + b], 1), :]
            spreadout = jnp.where(diagonal, values[b : b + 1, :], 0.0)
            spreadout -= cond[b, :, :width] * c0 + cond[b, :, width:] * c1
            rest = jnp.sum(spreadout, axis=1, keepdims=True)
            out = jnp.sum(both[b] * rest, axis=0, keepdims=True)
            own[b : b + 1, :] = out[:, :width]
            push[b : b + 1, :] = out[:, width : 2 * width]
            push[blocks + b : blocks + b + 1, :] = out[:, 2 * width :]
        rest = push[...]
        split = []
        for _ in range(3):
            piece = rest.astype(jnp.bfloat16)
            split.append(piece)
            rest = rest - piece.astype(jnp.float32)
        sent[turn] = jnp.dot(
            hot, jnp.concatenate(split, axis=0), preferred_element_type=jnp.float32
        )

    def pulled_coarse(turn):
        total = landed[turn].reshape(devices, ROWS, width).sum(axis=0)
        row = lax.broadcasted_iota(jnp.int32, (ROWS, width), 0)
        total = jnp.where(row < COARSE_DEV, total, 0.0)
        return jnp.concatenate(
            [total, jnp.zeros((blocks - ROWS, width), jnp.float32)], axis=0
        )

    def pulled_near(turn):
        return sent[turn, halo + blocks : halo + 2 * blocks] + near[turn, 0] + near[turn, 1]

    arrive_near(first)
    arrive_coarse(0, table.at[0])
    pushes(0, latent)
    second = give(2)
    known = own[...] + (latent - observed_ref[...]) / nugget_ref[...]
    arrive_near(second)
    half = momentum_ref[...] - 0.5 * leap_step * (known - pulled_near(0))
    fine[...] = latent + leap_step * half
    third = spread_near(1, fine)
    arrive_coarse(2, landed.at[0])
    half = half + 0.5 * leap_step * pulled_coarse(0)
    moved = latent + leap_step * half
    coarse[...] = moved[:ROWS]
    spread_coarse(1, coarse.at[pl.ds(0, COARSE_DEV)])
    half_ref[...] = half
    keep(1, moved)
    arrive_near(third)
    arrive_coarse(1, table.at[1])
    pushes(1, moved)
    fourth = give(3)
    known = own[...] + (moved - observed_ref[...]) / nugget_ref[...]
    arrive_near(fourth)
    known = known - pulled_near(1)
    arrive_coarse(3, landed.at[1])
    grad_ref[...] = known - pulled_coarse(1)
    drain(0, table.at[0], first)
    drain(2, landed.at[0], second)
    drain(1, table.at[1], third)
    drain(3, landed.at[1], fourth)


def on_device(latent, momentum, observed, nugget, cond_weights, whiten, slot_of_rank, neighbours):
    ngrp, ntile = lax.axis_size("grp"), lax.axis_size("tile")
    blocks, width = latent.shape
    devices = ngrp * ntile
    rows = devices * ROWS + 3 * blocks
    f32 = jnp.float32
    vmem = pl.BlockSpec(memory_space=pltpu.VMEM)
    anywhere = pl.BlockSpec(memory_space=pltpu.HBM)
    half, end_grad = pl.pallas_call(
        functools.partial(kernel, ngrp, ntile),
        out_shape=[jax.ShapeDtypeStruct((blocks, width), f32)] * 2,
        in_specs=[anywhere] * 8,
        out_specs=[vmem] * 2,
        scratch_shapes=[
            *[pltpu.VMEM((blocks, width), f32)] * 4,
            pltpu.SMEM(slot_of_rank.shape, jnp.int32),
            pltpu.SMEM((2, blocks), jnp.int32),
            pltpu.VMEM(cond_weights.shape, f32),
            pltpu.VMEM(whiten.shape, f32),
            pltpu.VMEM((blocks, width, 3 * width), f32),
            pltpu.VMEM((2, rows + ROWS, width), f32),
            pltpu.VMEM((2, rows, width), f32),
            pltpu.VMEM((2, devices * ROWS, width), f32),
            pltpu.VMEM((2, 2, blocks, width), f32),
            pltpu.VMEM((2 * blocks, width), f32),
            pltpu.VMEM((blocks, width), f32),
            pltpu.VMEM((blocks, width), f32),
            pltpu.VMEM((ROWS, width), f32),
            pltpu.SMEM((2 * blocks,), jnp.int32),
            pltpu.SemaphoreType.DMA((6,)),
            pltpu.SemaphoreType.DMA((2, 4)),
            pltpu.SemaphoreType.DMA((4,)),
            pltpu.SemaphoreType.DMA((4,)),
            pltpu.SemaphoreType.DMA((4, 2, 2)),
        ],
        compiler_params=pltpu.CompilerParams(
            collective_id=0, has_side_effects=True, vmem_limit_bytes=60 * 1024 * 1024
        ),
    )(latent, momentum, observed, nugget, cond_weights, whiten, slot_of_rank, neighbours.T)
    return latent + leap_step * half, half - 0.5 * leap_step * end_grad


def solution(mesh):
    split = P(("grp", "tile"), None)
    cube = P(("grp", "tile"), None, None)
    return jax.shard_map(
        on_device,
        mesh=mesh,
        in_specs=(split, split, split, split, cube, cube, P(), split),
        out_specs=(split, split),
        check_vma=False,
    )
```

```python
import functools

import jax
import jax.numpy as jnp
from jax import lax
from jax.experimental import pallas as pl
from jax.experimental.pallas import tpu as pltpu
from jax.sharding import PartitionSpec as P

COARSE_DEV = 2
ROWS = 8

leap_step = 0.25

MESH = pl.DeviceIdType.MESH


def halves(x):
    high = x.astype(jnp.bfloat16)
    return high, (x - high.astype(jnp.float32)).astype(jnp.bfloat16)


def kernel(
    ngrp,
    ntile,
    latent_hbm,
    momentum_hbm,
    observed_hbm,
    nugget_hbm,
    cond_hbm,
    whiten_hbm,
    slot_hbm,
    neigh_hbm,
    half_ref,
    grad_ref,
    latent_ref,
    momentum_ref,
    observed_ref,
    nugget_ref,
    slot_ref,
    neigh_ref,
    cond,
    whit,
    both,
    table,
    sent,
    landed,
    near,
    push,
    own,
    fine,
    coarse,
    index,
    small_sem,
    load_sem,
    send_sem,
    recv_sem,
    near_sem,
):
    blocks, width = latent_ref.shape
    devices = ngrp * ntile
    grp = lax.axis_index("grp")
    tile = lax.axis_index("tile")
    me = grp * ntile + tile
    halo = devices * ROWS
    absent = halo + 3 * blocks
    above = (grp, lax.rem(tile + 1, ntile))
    below = (grp, lax.rem(tile + ntile - 1, ntile))

    def everyone(act):
        if devices <= 64:
            groups = [lax.rem(grp + a, ngrp) for a in range(ngrp)]
            tiles = [lax.rem(tile + b, ntile) for b in range(ntile)]
            for a in [*range(1, ngrp), 0]:
                for b in reversed(range(ntile)):
                    if a or b:
                        act(groups[a] * ntile + tiles[b], (groups[a], tiles[b]))
        else:

            def body(step, carry):
                flat = lax.rem(me + step, devices)
                act(flat, (flat // ntile, lax.rem(flat, ntile)))
                return carry

            lax.fori_loop(1, devices, body, 0)

    barrier = pltpu.get_barrier_semaphore()

    def greet(flat, to):
        pl.semaphore_signal(barrier, inc=1, device_id=to, device_id_type=MESH)

    everyone(greet)

    small = [
        pltpu.make_async_copy(source, target, small_sem.at[i])
        for i, (source, target) in enumerate(
            (
                (neigh_hbm, neigh_ref),
                (slot_hbm, slot_ref),
                (latent_hbm, latent_ref),
                (momentum_hbm, momentum_ref),
                (observed_hbm, observed_ref),
                (nugget_hbm, nugget_ref),
            )
        )
    ]
    for copy in small:
        copy.start()
    loads = []
    pieces = load_sem.shape[1]
    part = blocks // pieces
    for i in range(pieces):
        rows = pl.ds(i * part, part)
        loads.append(
            (
                pltpu.make_async_copy(whiten_hbm.at[rows], whit.at[rows], load_sem.at[0, i]),
                pltpu.make_async_copy(cond_hbm.at[rows], cond.at[rows], load_sem.at[1, i]),
            )
        )
    for pair in loads:
        for copy in pair:
            copy.start()

    pl.semaphore_wait(barrier, devices - 1)

    my_rows = pl.ds(pl.multiple_of(me * ROWS, ROWS), COARSE_DEV)

    def spread_coarse(turn, values):
        def send(flat, to):
            pltpu.make_async_remote_copy(
                src_ref=values,
                dst_ref=table.at[turn, my_rows],
                send_sem=send_sem.at[turn],
                recv_sem=recv_sem.at[turn],
                device_id=to,
                device_id_type=MESH,
            ).start()

        everyone(send)

    def spread_near(turn, values):
        sends = []
        for side, (to, row) in enumerate(((above, halo), (below, halo + 2 * blocks))):
            copy = pltpu.make_async_remote_copy(
                src_ref=values,
                dst_ref=table.at[turn, pl.ds(row, blocks)],
                send_sem=near_sem.at[turn, 0, side],
                recv_sem=near_sem.at[turn, 1, side],
                device_id=to,
                device_id_type=MESH,
            )
            copy.start()
            sends.append(copy)
        return sends

    def give(turn):
        def send(flat, to):
            pltpu.make_async_remote_copy(
                src_ref=sent.at[turn - 2, pl.ds(pl.multiple_of(flat * ROWS, ROWS), COARSE_DEV)],
                dst_ref=landed.at[turn - 2, my_rows],
                send_sem=send_sem.at[turn],
                recv_sem=recv_sem.at[turn],
                device_id=to,
                device_id_type=MESH,
            ).start()

        everyone(send)
        sends = []
        for side, (to, row) in enumerate(((above, halo + 2 * blocks), (below, halo))):
            copy = pltpu.make_async_remote_copy(
                src_ref=sent.at[turn - 2, pl.ds(row, blocks)],
                dst_ref=near.at[turn - 2, side],
                send_sem=near_sem.at[turn, 0, side],
                recv_sem=near_sem.at[turn, 1, side],
                device_id=to,
                device_id_type=MESH,
            )
            copy.start()
            sends.append(copy)
        mine = pl.ds(pl.multiple_of(me * ROWS, ROWS), ROWS)
        landed[turn - 2, mine] = sent[turn - 2, mine]
        return sends

    def arrive_near(sends):
        for copy in sends:
            copy.wait_recv()

    def arrive_coarse(turn, buffer):
        amount = buffer.at[pl.ds(0, (devices - 1) * COARSE_DEV)]
        pltpu.make_async_copy(amount, amount, recv_sem.at[turn]).wait()

    def drain(turn, buffer, sends):
        for copy in sends:
            copy.wait_send()
        amount = buffer.at[pl.ds(0, (devices - 1) * COARSE_DEV)]
        pltpu.make_async_copy(amount, amount, send_sem.at[turn]).wait()

    def keep(turn, values):
        table[turn, my_rows] = values[:COARSE_DEV]
        table[turn, halo + blocks : halo + 2 * blocks] = values

    spread_coarse(0, latent_hbm.at[pl.ds(0, COARSE_DEV)])
    first = spread_near(0, latent_hbm)
    small[0].wait()
    small[1].wait()
    lanes = lax.broadcasted_iota(jnp.int32, (1, 6 * blocks), 1) % (2 * blocks)
    places = jnp.full((1, 6 * blocks), -1, jnp.int32)
    for s in range(blocks):
        for k in range(2):
            rank = neigh_ref[k, s]
            slot = slot_ref[rank]
            owner = slot // blocks
            place = lax.rem(slot, blocks)
            row = jnp.where(
                rank < COARSE_DEV * devices,
                owner * ROWS + place,
                halo + (owner - me + 1) * blocks + place,
            )
            row = jnp.where(slot == me * blocks + s, absent, row)
            index[k * blocks + s] = row
            places = jnp.where(lanes == k * blocks + s, row, places)
    hot = (lax.broadcasted_iota(jnp.int32, (absent, 6 * blocks), 0) == places)
    hot = hot.astype(jnp.float32).astype(jnp.bfloat16)
    for turn in range(2):
        table[turn, absent : absent + ROWS] = jnp.zeros((ROWS, width), jnp.float32)

    for copy in small[2:]:
        copy.wait()
    latent = latent_ref[...]
    keep(0, latent)

    for i, pair in enumerate(loads):
        for copy in pair:
            copy.wait()
        for b in range(i * part, (i + 1) * part):
            high, low = halves(whit[b])
            square = lax.dot_general(
                jnp.concatenate([high, high, low], axis=0),
                jnp.concatenate([high, low, high], axis=0),
                (((0,), (0,)), ((), ())),
                preferred_element_type=jnp.float32,
            )
            both[b, :, :width] = square
            left_high, left_low = halves(square)
            high, low = halves(cond[b])
            both[b, :, width:] = jnp.dot(
                jnp.concatenate([left_high, left_high, left_low], axis=1),
                jnp.concatenate([high, low, high], axis=0),
                preferred_element_type=jnp.float32,
            )

    diagonal = lax.broadcasted_iota(jnp.int32, (width, width), 0) == lax.broadcasted_iota(
        jnp.int32, (width, width), 1
    )

    def pushes(turn, values):
        for b in range(blocks):
            c0 = table[turn, pl.ds(index[b], 1), :]
            c1 = table[turn, pl.ds(index[blocks + b], 1), :]
            spreadout = jnp.where(diagonal, values[b : b + 1, :], 0.0)
            spreadout -= cond[b, :, :width] * c0 + cond[b, :, width:] * c1
            rest = jnp.sum(spreadout, axis=1, keepdims=True)
            out = jnp.sum(both[b] * rest, axis=0, keepdims=True)
            own[b : b + 1, :] = out[:, :width]
            push[b : b + 1, :] = out[:, width : 2 * width]
            push[blocks + b : blocks + b + 1, :] = out[:, 2 * width :]
        rest = push[...]
        split = []
        for _ in range(3):
            piece = rest.astype(jnp.bfloat16)
            split.append(piece)
            rest = rest - piece.astype(jnp.float32)
        sent[turn] = jnp.dot(
            hot, jnp.concatenate(split, axis=0), preferred_element_type=jnp.float32
        )

    def pulled_coarse(turn):
        total = landed[turn].reshape(devices, ROWS, width).sum(axis=0)
        row = lax.broadcasted_iota(jnp.int32, (ROWS, width), 0)
        total = jnp.where(row < COARSE_DEV, total, 0.0)
        return jnp.concatenate(
            [total, jnp.zeros((blocks - ROWS, width), jnp.float32)], axis=0
        )

    def pulled_near(turn):
        return sent[turn, halo + blocks : halo + 2 * blocks] + near[turn, 0] + near[turn, 1]

    arrive_near(first)
    arrive_coarse(0, table.at[0])
    pushes(0, latent)
    second = give(2)
    known = own[...] + (latent - observed_ref[...]) / nugget_ref[...]
    arrive_near(second)
    half = momentum_ref[...] - 0.5 * leap_step * (known - pulled_near(0))
    fine[...] = latent + leap_step * half
    third = spread_near(1, fine)
    arrive_coarse(2, landed.at[0])
    half = half + 0.5 * leap_step * pulled_coarse(0)
    moved = latent + leap_step * half
    coarse[...] = moved[:ROWS]
    spread_coarse(1, coarse.at[pl.ds(0, COARSE_DEV)])
    half_ref[...] = half
    keep(1, moved)
    arrive_near(third)
    arrive_coarse(1, table.at[1])
    pushes(1, moved)
    fourth = give(3)
    known = own[...] + (moved - observed_ref[...]) / nugget_ref[...]
    arrive_near(fourth)
    known = known - pulled_near(1)
    arrive_coarse(3, landed.at[1])
    grad_ref[...] = known - pulled_coarse(1)
    drain(0, table.at[0], first)
    drain(2, landed.at[0], second)
    drain(1, table.at[1], third)
    drain(3, landed.at[1], fourth)


def on_device(latent, momentum, observed, nugget, cond_weights, whiten, slot_of_rank, neighbours):
    ngrp, ntile = lax.axis_size("grp"), lax.axis_size("tile")
    blocks, width = latent.shape
    devices = ngrp * ntile
    rows = devices * ROWS + 3 * blocks
    f32 = jnp.float32
    vmem = pl.BlockSpec(memory_space=pltpu.VMEM)
    anywhere = pl.BlockSpec(memory_space=pltpu.HBM)
    half, end_grad = pl.pallas_call(
        functools.partial(kernel, ngrp, ntile),
        out_shape=[pltpu.VMEM((blocks, width), f32)] * 2,
        in_specs=[anywhere] * 8,
        out_specs=[vmem] * 2,
        scratch_shapes=[
            *[pltpu.VMEM((blocks, width), f32)] * 4,
            pltpu.SMEM(slot_of_rank.shape, jnp.int32),
            pltpu.SMEM((2, blocks), jnp.int32),
            pltpu.VMEM(cond_weights.shape, f32),
            pltpu.VMEM(whiten.shape, f32),
            pltpu.VMEM((blocks, width, 3 * width), f32),
            pltpu.VMEM((2, rows + ROWS, width), f32),
            pltpu.VMEM((2, rows, width), f32),
            pltpu.VMEM((2, devices * ROWS, width), f32),
            pltpu.VMEM((2, 2, blocks, width), f32),
            pltpu.VMEM((2 * blocks, width), f32),
            pltpu.VMEM((blocks, width), f32),
            pltpu.VMEM((blocks, width), f32),
            pltpu.VMEM((ROWS, width), f32),
            pltpu.SMEM((2 * blocks,), jnp.int32),
            pltpu.SemaphoreType.DMA((6,)),
            pltpu.SemaphoreType.DMA((2, 4)),
            pltpu.SemaphoreType.DMA((4,)),
            pltpu.SemaphoreType.DMA((4,)),
            pltpu.SemaphoreType.DMA((4, 2, 2)),
        ],
        compiler_params=pltpu.CompilerParams(
            collective_id=0, has_side_effects=True, vmem_limit_bytes=60 * 1024 * 1024
        ),
    )(latent, momentum, observed, nugget, cond_weights, whiten, slot_of_rank, neighbours.T)
    return latent + leap_step * half, half - 0.5 * leap_step * end_grad


def solution(mesh):
    split = P(("grp", "tile"), None)
    cube = P(("grp", "tile"), None, None)
    return jax.shard_map(
        on_device,
        mesh=mesh,
        in_specs=(split, split, split, split, cube, cube, P(), split),
        out_specs=(split, split),
        check_vma=False,
    )
```

```python
import functools

import jax
import jax.numpy as jnp
from jax import lax
from jax.experimental import pallas as pl
from jax.experimental.pallas import tpu as pltpu
from jax.sharding import PartitionSpec as P

COARSE_DEV = 2
ROWS = 8

leap_step = 0.25

MESH = pl.DeviceIdType.MESH


def halves(x):
    high = x.astype(jnp.bfloat16)
    return high, (x - high.astype(jnp.float32)).astype(jnp.bfloat16)


def kernel(
    ngrp,
    ntile,
    latent_hbm,
    momentum_hbm,
    observed_hbm,
    nugget_hbm,
    cond_hbm,
    whiten_hbm,
    slot_hbm,
    neigh_hbm,
    half_ref,
    grad_ref,
    latent_ref,
    momentum_ref,
    observed_ref,
    nugget_ref,
    slot_ref,
    neigh_ref,
    cond,
    whit,
    both,
    table,
    sent,
    landed,
    near,
    push,
    own,
    fine,
    coarse,
    index,
    small_sem,
    load_sem,
    send_sem,
    recv_sem,
    near_sem,
):
    blocks, width = latent_ref.shape
    devices = ngrp * ntile
    grp = lax.axis_index("grp")
    tile = lax.axis_index("tile")
    me = grp * ntile + tile
    halo = devices * ROWS
    absent = halo + 3 * blocks
    above = (grp, lax.rem(tile + 1, ntile))
    below = (grp, lax.rem(tile + ntile - 1, ntile))

    def everyone(act):
        if devices <= 64:
            groups = [lax.rem(grp + a, ngrp) for a in range(ngrp)]
            tiles = [lax.rem(tile + b, ntile) for b in range(ntile)]
            for a in [*range(1, ngrp), 0]:
                for b in reversed(range(ntile)):
                    if a or b:
                        act(groups[a] * ntile + tiles[b], (groups[a], tiles[b]))
        else:

            def body(step, carry):
                flat = lax.rem(me + step, devices)
                act(flat, (flat // ntile, lax.rem(flat, ntile)))
                return carry

            lax.fori_loop(1, devices, body, 0)

    barrier = pltpu.get_barrier_semaphore()

    def greet(flat, to):
        pl.semaphore_signal(barrier, inc=1, device_id=to, device_id_type=MESH)

    everyone(greet)

    small = [
        pltpu.make_async_copy(source, target, small_sem.at[i])
        for i, (source, target) in enumerate(
            (
                (neigh_hbm, neigh_ref),
                (slot_hbm, slot_ref),
                (latent_hbm, latent_ref),
                (momentum_hbm, momentum_ref),
                (observed_hbm, observed_ref),
                (nugget_hbm, nugget_ref),
            )
        )
    ]
    for copy in small:
        copy.start()
    loads = []
    pieces = load_sem.shape[1]
    part = blocks // pieces
    for i in range(pieces):
        rows = pl.ds(i * part, part)
        loads.append(
            (
                pltpu.make_async_copy(whiten_hbm.at[rows], whit.at[rows], load_sem.at[0, i]),
                pltpu.make_async_copy(cond_hbm.at[rows], cond.at[rows], load_sem.at[1, i]),
            )
        )
    for pair in loads:
        for copy in pair:
            copy.start()

    pl.semaphore_wait(barrier, devices - 1)

    my_rows = pl.ds(pl.multiple_of(me * ROWS, ROWS), COARSE_DEV)

    def spread_coarse(turn, values):
        def send(flat, to):
            pltpu.make_async_remote_copy(
                src_ref=values,
                dst_ref=table.at[turn, my_rows],
                send_sem=send_sem.at[turn],
                recv_sem=recv_sem.at[turn],
                device_id=to,
                device_id_type=MESH,
            ).start()

        everyone(send)

    def spread_near(turn, values):
        sends = []
        for side, (to, row) in enumerate(((above, halo), (below, halo + 2 * blocks))):
            copy = pltpu.make_async_remote_copy(
                src_ref=values,
                dst_ref=table.at[turn, pl.ds(row, blocks)],
                send_sem=near_sem.at[turn, 0, side],
                recv_sem=near_sem.at[turn, 1, side],
                device_id=to,
                device_id_type=MESH,
            )
            copy.start()
            sends.append(copy)
        return sends

    def give(turn, split):
        sent[turn - 2, :halo] = jnp.dot(hot[:halo], split, preferred_element_type=jnp.float32)

        def send(flat, to):
            pltpu.make_async_remote_copy(
                src_ref=sent.at[turn - 2, pl.ds(pl.multiple_of(flat * ROWS, ROWS), COARSE_DEV)],
                dst_ref=landed.at[turn - 2, my_rows],
                send_sem=send_sem.at[turn],
                recv_sem=recv_sem.at[turn],
                device_id=to,
                device_id_type=MESH,
            ).start()

        everyone(send)
        sent[turn - 2, halo:] = jnp.dot(hot[halo:], split, preferred_element_type=jnp.float32)
        sends = []
        for side, (to, row) in enumerate(((above, halo + 2 * blocks), (below, halo))):
            copy = pltpu.make_async_remote_copy(
                src_ref=sent.at[turn - 2, pl.ds(row, blocks)],
                dst_ref=near.at[turn - 2, side],
                send_sem=near_sem.at[turn, 0, side],
                recv_sem=near_sem.at[turn, 1, side],
                device_id=to,
                device_id_type=MESH,
            )
            copy.start()
            sends.append(copy)
        mine = pl.ds(pl.multiple_of(me * ROWS, ROWS), ROWS)
        landed[turn - 2, mine] = sent[turn - 2, mine]
        return sends

    def arrive_near(sends):
        for copy in sends:
            copy.wait_recv()

    def arrive_coarse(turn, buffer):
        amount = buffer.at[pl.ds(0, (devices - 1) * COARSE_DEV)]
        pltpu.make_async_copy(amount, amount, recv_sem.at[turn]).wait()

    def drain(turn, buffer, sends):
        for copy in sends:
            copy.wait_send()
        amount = buffer.at[pl.ds(0, (devices - 1) * COARSE_DEV)]
        pltpu.make_async_copy(amount, amount, send_sem.at[turn]).wait()

    def keep(turn, values):
        table[turn, my_rows] = values[:COARSE_DEV]
        table[turn, halo + blocks : halo + 2 * blocks] = values

    spread_coarse(0, latent_hbm.at[pl.ds(0, COARSE_DEV)])
    first = spread_near(0, latent_hbm)
    small[0].wait()
    small[1].wait()
    lanes = lax.broadcasted_iota(jnp.int32, (1, 6 * blocks), 1) % (2 * blocks)
    places = jnp.full((1, 6 * blocks), -1, jnp.int32)
    for s in range(blocks):
        for k in range(2):
            rank = neigh_ref[k, s]
            slot = slot_ref[rank]
            owner = slot // blocks
            place = lax.rem(slot, blocks)
            row = jnp.where(
                rank < COARSE_DEV * devices,
                owner * ROWS + place,
                halo + (owner - me + 1) * blocks + place,
            )
            row = jnp.where(slot == me * blocks + s, absent, row)
            index[k * blocks + s] = row
            places = jnp.where(lanes == k * blocks + s, row, places)
    hot = (lax.broadcasted_iota(jnp.int32, (absent, 6 * blocks), 0) == places)
    hot = hot.astype(jnp.float32).astype(jnp.bfloat16)
    for turn in range(2):
        table[turn, absent : absent + ROWS] = jnp.zeros((ROWS, width), jnp.float32)

    for copy in small[2:]:
        copy.wait()
    latent = latent_ref[...]
    keep(0, latent)

    for i, pair in enumerate(loads):
        for copy in pair:
            copy.wait()
        for b in range(i * part, (i + 1) * part):
            high, low = halves(whit[b])
            square = lax.dot_general(
                jnp.concatenate([high, high, low], axis=0),
                jnp.concatenate([high, low, high], axis=0),
                (((0,), (0,)), ((), ())),
                preferred_element_type=jnp.float32,
            )
            both[b, :, :width] = square
            left_high, left_low = halves(square)
            high, low = halves(cond[b])
            both[b, :, width:] = jnp.dot(
                jnp.concatenate([left_high, left_high, left_low], axis=1),
                jnp.concatenate([high, low, high], axis=0),
                preferred_element_type=jnp.float32,
            )

    diagonal = lax.broadcasted_iota(jnp.int32, (width, width), 0) == lax.broadcasted_iota(
        jnp.int32, (width, width), 1
    )

    def pushes(turn, values):
        for b in range(blocks):
            c0 = table[turn, pl.ds(index[b], 1), :]
            c1 = table[turn, pl.ds(index[blocks + b], 1), :]
            spreadout = jnp.where(diagonal, values[b : b + 1, :], 0.0)
            spreadout -= cond[b, :, :width] * c0 + cond[b, :, width:] * c1
            rest = jnp.sum(spreadout, axis=1, keepdims=True)
            out = jnp.sum(both[b] * rest, axis=0, keepdims=True)
            own[b : b + 1, :] = out[:, :width]
            push[b : b + 1, :] = out[:, width : 2 * width]
            push[blocks + b : blocks + b + 1, :] = out[:, 2 * width :]
        rest = push[...]
        split = []
        for _ in range(3):
            piece = rest.astype(jnp.bfloat16)
            split.append(piece)
            rest = rest - piece.astype(jnp.float32)
        return jnp.concatenate(split, axis=0)

    def pulled_coarse(turn):
        total = landed[turn].reshape(devices, ROWS, width).sum(axis=0)
        row = lax.broadcasted_iota(jnp.int32, (ROWS, width), 0)
        total = jnp.where(row < COARSE_DEV, total, 0.0)
        return jnp.concatenate(
            [total, jnp.zeros((blocks - ROWS, width), jnp.float32)], axis=0
        )

    def pulled_near(turn):
        return sent[turn, halo + blocks : halo + 2 * blocks] + near[turn, 0] + near[turn, 1]

    arrive_near(first)
    arrive_coarse(0, table.at[0])
    second = give(2, pushes(0, latent))
    known = own[...] + (latent - observed_ref[...]) / nugget_ref[...]
    arrive_near(second)
    half = momentum_ref[...] - 0.5 * leap_step * (known - pulled_near(0))
    fine[...] = latent + leap_step * half
    third = spread_near(1, fine)
    arrive_coarse(2, landed.at[0])
    half = half + 0.5 * leap_step * pulled_coarse(0)
    moved = latent + leap_step * half
    coarse[...] = moved[:ROWS]
    spread_coarse(1, coarse.at[pl.ds(0, COARSE_DEV)])
    half_ref[...] = half
    keep(1, moved)
    arrive_near(third)
    arrive_coarse(1, table.at[1])
    fourth = give(3, pushes(1, moved))
    known = own[...] + (moved - observed_ref[...]) / nugget_ref[...]
    arrive_near(fourth)
    known = known - pulled_near(1)
    arrive_coarse(3, landed.at[1])
    grad_ref[...] = known - pulled_coarse(1)
    drain(0, table.at[0], first)
    drain(2, landed.at[0], second)
    drain(1, table.at[1], third)
    drain(3, landed.at[1], fourth)


def on_device(latent, momentum, observed, nugget, cond_weights, whiten, slot_of_rank, neighbours):
    ngrp, ntile = lax.axis_size("grp"), lax.axis_size("tile")
    blocks, width = latent.shape
    devices = ngrp * ntile
    rows = devices * ROWS + 3 * blocks
    f32 = jnp.float32
    vmem = pl.BlockSpec(memory_space=pltpu.VMEM)
    anywhere = pl.BlockSpec(memory_space=pltpu.HBM)
    half, end_grad = pl.pallas_call(
        functools.partial(kernel, ngrp, ntile),
        out_shape=[pltpu.VMEM((blocks, width), f32)] * 2,
        in_specs=[anywhere] * 8,
        out_specs=[vmem] * 2,
        scratch_shapes=[
            *[pltpu.VMEM((blocks, width), f32)] * 4,
            pltpu.SMEM(slot_of_rank.shape, jnp.int32),
            pltpu.SMEM((2, blocks), jnp.int32),
            pltpu.VMEM(cond_weights.shape, f32),
            pltpu.VMEM(whiten.shape, f32),
            pltpu.VMEM((blocks, width, 3 * width), f32),
            pltpu.VMEM((2, rows + ROWS, width), f32),
            pltpu.VMEM((2, rows, width), f32),
            pltpu.VMEM((2, devices * ROWS, width), f32),
            pltpu.VMEM((2, 2, blocks, width), f32),
            pltpu.VMEM((2 * blocks, width), f32),
            pltpu.VMEM((blocks, width), f32),
            pltpu.VMEM((blocks, width), f32),
            pltpu.VMEM((ROWS, width), f32),
            pltpu.SMEM((2 * blocks,), jnp.int32),
            pltpu.SemaphoreType.DMA((6,)),
            pltpu.SemaphoreType.DMA((2, 4)),
            pltpu.SemaphoreType.DMA((4,)),
            pltpu.SemaphoreType.DMA((4,)),
            pltpu.SemaphoreType.DMA((4, 2, 2)),
        ],
        compiler_params=pltpu.CompilerParams(
            collective_id=0, has_side_effects=True, vmem_limit_bytes=60 * 1024 * 1024
        ),
    )(latent, momentum, observed, nugget, cond_weights, whiten, slot_of_rank, neighbours.T)
    return latent + leap_step * half, half - 0.5 * leap_step * end_grad


def solution(mesh):
    split = P(("grp", "tile"), None)
    cube = P(("grp", "tile"), None, None)
    return jax.shard_map(
        on_device,
        mesh=mesh,
        in_specs=(split, split, split, split, cube, cube, P(), split),
        out_specs=(split, split),
        check_vma=False,
    )
```
